256 devices in a mesh: group: 4 (over y), dev: 64 (over z, x, core).
Axes of the slice: x: 4, y: 4, z: 8, core: 2. Of those that a mesh axis runs over, the one named last changes fastest.
Arguments:
- history: bfloat16 [256, 48, 64, 256], P(('group', 'dev')), may hold values from -6 to 6
- incident: float32 [256, 3, 64, 256], P(('group', 'dev')), may hold values from -6 to 6
- jacobi: float32 [256, 256, 256], P(('group', 'dev')), may hold values from -0.375 to 0.375
- self_tiles: bfloat16 [256, 2, 256, 256], P(('group', 'dev')), may hold values from -0.25 to 0.25
- near_tiles: bfloat16 [256, 76, 256, 256], P(('group', 'dev')), may hold values from -0.0390625 to 0.0390625
- send_lag: int32 [256, 64, 1], P(('group', 'dev')), may hold values from 3 to 48
- cross_lag: int32 [256, 4, 2], P(('group', 'dev')), may hold values from 3 to 48
- tile_slot: int32 [256, 76], P(('group', 'dev')), may hold values from 0 to 71, as said below
- tile_dest: int32 [256, 76], P(('group', 'dev')), may hold values from 0 to 63
Outputs:
- solution: float32 [256, 3, 64, 256], P(('group', 'dev'))
The draws below stay inside these ranges and needn't reach their ends.
Inputs may be any that keep to these rules, and one draw needn't show every extreme that they name: `tile_slot`: every slot index 0 .. 71 is read by at least one tile of every device; the other tiles read any slot.
All inputs are finite; a program needn't handle non-finite values.
Results may differ from the reference program's by a relative error of at most 0.0022.
Values may be sent and summed in bfloat16 or wider, within the bound.
A program may use at most 128 MiB of HBM per device.

```python
import jax
import jax.numpy as jnp
from jax import lax

P_SIZE = 256
R = 64
LAGS = 48
STEPS = 3
SLOTS = 1
GSLOTS = 2
SURPLUS_TILES = 4
PANEL_BLOCKS = 256
HISTORY_COUNT = 72
TILES_DEV = 76
N_GROUP = 4
N_DEV = 64


def draw_tile_slot(key, part):
    keys = jax.random.split(jax.random.fold_in(key, 11), PANEL_BLOCKS)
    surplus_key = jax.random.fold_in(key, 12)
    surplus_tile = jax.random.randint(surplus_key, (PANEL_BLOCKS, SURPLUS_TILES), 0, HISTORY_COUNT)

    def one_row(row_key, row_surplus):
        base_offset = jnp.concatenate([jnp.arange(HISTORY_COUNT, dtype=jnp.int32), row_surplus.astype(jnp.int32)])
        return jax.random.permutation(row_key, base_offset)
    return jax.vmap(one_row)(keys, surplus_tile).astype(jnp.int32)


def with_ends(entries, own_key, least, high):
    extent = entries.shape
    spot = [jax.random.randint(jax.random.fold_in(own_key, axis), (), 0, extent[axis]) for axis in range(len(extent))]
    entries = entries.at[tuple(spot)].set(least)
    longest = extent.index(max(extent))
    spot[longest] = (spot[longest] + 1) % extent[longest]
    return entries.at[tuple(spot)].set(high)


def levels(stream_key, extent, cuts, low, high):
    factor_of, own = 1.0, jax.random.fold_in(stream_key, 6)
    for dim, shards_of in cuts:
        heights = jnp.exp(jax.random.uniform(jax.random.fold_in(own, dim), (shards_of,), jnp.float32, low / len(cuts), high / len(cuts)))
        factor_of = factor_of * jnp.repeat(heights, extent[dim] // shards_of).reshape([-1 if axis == dim else 1 for axis in range(len(extent))])
    return factor_of


def bell_draw(rng, shape, scale, most, pieces=(), kind=jnp.bfloat16):
    result = scale * jax.random.normal(rng, shape, jnp.float32)
    if pieces:
        result = result * levels(rng, shape, pieces, -0.22, 0.18)
    return jnp.clip(result, -most, most).astype(kind)


def setup_inputs(seed: int = 0) -> dict:
    arg_keys = jax.random.split(jax.random.key(seed), 10)
    history = bell_draw(arg_keys[0], (PANEL_BLOCKS, LAGS, R, P_SIZE), 1.0, 6.0, ((0, 256),))
    incident = bell_draw(arg_keys[1], (PANEL_BLOCKS, STEPS, R, P_SIZE), 1.0, 6.0, ((0, 256),), jnp.float32)
    jacobi = bell_draw(arg_keys[2], (PANEL_BLOCKS, P_SIZE, P_SIZE), P_SIZE ** -0.5, 0.375, ((0, 256),), jnp.float32)
    self_tiles = bell_draw(arg_keys[3], (PANEL_BLOCKS, 2, P_SIZE, P_SIZE), (2 * P_SIZE) ** -0.5, 0.25, ((0, 256),))
    near_tiles = bell_draw(arg_keys[4], (PANEL_BLOCKS, TILES_DEV, P_SIZE, P_SIZE), (P_SIZE * TILES_DEV) ** -0.5, 0.0390625, ((0, 256),))
    send_lag = with_ends(jax.random.randint(arg_keys[5], (PANEL_BLOCKS, N_DEV, SLOTS), 3, LAGS + 1), jax.random.fold_in(arg_keys[5], 1), 3, LAGS).astype(jnp.int32)
    cross_lag = with_ends(jax.random.randint(arg_keys[6], (PANEL_BLOCKS, N_GROUP, GSLOTS), 3, LAGS + 1), jax.random.fold_in(arg_keys[6], 1), 3, LAGS).astype(jnp.int32)
    tile_slot = draw_tile_slot(jax.random.fold_in(arg_keys[9], 71), 0)
    tile_dest = with_ends(jax.random.randint(arg_keys[8], (PANEL_BLOCKS, TILES_DEV), 0, N_DEV), jax.random.fold_in(arg_keys[8], 1), 0, N_DEV - 1).astype(jnp.int32)
    return {"history": history, "incident": incident, "jacobi": jacobi, "self_tiles": self_tiles, "near_tiles": near_tiles, "send_lag": send_lag, "cross_lag": cross_lag, "tile_slot": tile_slot, "tile_dest": tile_dest}


def received_blocks(history, send_lag, cross_lag, step):
    hist = history.reshape(N_GROUP, N_DEV, LAGS, R, P_SIZE)
    lag_in = send_lag.reshape(N_GROUP, N_DEV, N_DEV, SLOTS) - step - 1
    gidx = jnp.arange(N_GROUP, dtype=jnp.int32)[:, None, None, None]
    pidx = jnp.arange(N_DEV, dtype=jnp.int32)[None, :, None, None]
    inner = hist[gidx, pidx, lag_in.astype(jnp.int32)]
    inner = jnp.transpose(inner, (0, 2, 1, 3, 4, 5)).reshape(PANEL_BLOCKS, N_DEV * SLOTS, R, P_SIZE)
    lag_x = cross_lag.reshape(N_GROUP, N_DEV, N_GROUP, GSLOTS) - step - 1
    hidx = jnp.arange(N_GROUP, dtype=jnp.int32)[:, None, None, None]
    didx = jnp.arange(N_DEV, dtype=jnp.int32)[None, :, None, None]
    outer = hist[hidx, didx, lag_x.astype(jnp.int32)]
    outer = jnp.transpose(outer, (2, 1, 0, 3, 4, 5)).reshape(PANEL_BLOCKS, N_GROUP * GSLOTS, R, P_SIZE)
    return jnp.concatenate([inner, outer], axis=1)


def remote_step(received, near_tiles, tile_slot, tile_dest):
    def one_block(carry, inputs):
        recv_b, tiles_b, slot_b, dest_b, index = inputs
        vals = recv_b[slot_b].astype(jnp.float32)
        prod = jnp.einsum('trp,tpq->trq', vals, tiles_b.astype(jnp.float32))
        group = index // N_DEV
        target = (group * N_DEV + dest_b).astype(jnp.int32)
        return carry.at[target].add(prod), None

    start = jnp.zeros((PANEL_BLOCKS, R, P_SIZE), jnp.float32)
    indices = jnp.arange(PANEL_BLOCKS, dtype=jnp.int32)
    total, _ = lax.scan(one_block, start, (received, near_tiles, tile_slot, tile_dest, indices))
    return total


def reference(history, incident, jacobi, self_tiles, near_tiles, send_lag, cross_lag, tile_slot, tile_dest):
    remote = []
    for step in range(STEPS):
        received = received_blocks(history, send_lag, cross_lag, step)
        remote.append(remote_step(received, near_tiles, tile_slot, tile_dest))
    first_tile = self_tiles[:, 0].astype(jnp.float32)
    second_tile = self_tiles[:, 1].astype(jnp.float32)
    prior_one = history[:, 0]
    prior_two = history[:, 1]
    solved = []
    for step in range(STEPS):
        selfterm = jnp.einsum('brp,bpq->brq', prior_one.astype(jnp.float32), first_tile)
        selfterm = selfterm + jnp.einsum('brp,bpq->brq', prior_two.astype(jnp.float32), second_tile)
        resid = incident[:, step] - remote[step] - selfterm
        value = jnp.einsum('brp,bpq->brq', resid, jacobi, precision=lax.Precision.HIGHEST)
        solved.append(value)
        prior_two = prior_one
        prior_one = value.astype(jnp.bfloat16)
    return jnp.stack(solved, axis=1)
```

```python
import functools

import jax
import jax.numpy as jnp
from jax import lax
from jax.experimental import pallas as pl
from jax.experimental.pallas import tpu as pltpu
from jax.sharding import PartitionSpec as P

MESH = pl.DeviceIdType.MESH
Z, X, C = 8, 4, 2
S = X * C
G = 4
LAGS, R, W, STEPS = 48, 64, 256, 3
TILES = 76
SLOTS = Z * S + 2 * G
CH = 4
RC = R // CH
ROWS = STEPS * RC
F32, BF16, I32 = jnp.float32, jnp.bfloat16, jnp.int32
SEND1, SEND2, SEND3 = F32, BF16, BF16
UNROLL = 4


def kernel(
    meta, hist, inc_hbm, jac_hbm, self_hbm, tiles_hbm, out,
    hists, pkt3, pkt4, fsel, sel, csel, recvs, tiles, inc, jac, selft,
    cum, send1, r1, send2, own2, r2, send3, own3, r3,
    lagbuf, srt, slag, ssrt,
    load_sem, in_sem, lag_s, lag_r, small_sem,
    h_s, h_r, x_s, x_r, rs_s, rs_r,
):
    dev, g = lax.axis_index("dev"), lax.axis_index("group")
    z, x, c = dev // S, (dev // C) % X, dev % C
    me = x * C + c

    def at(zz, xx, cc):
        return (g, (zz * X + xx) * C + cc)

    def zpeer(dz):
        return at(lax.rem(z + dz + Z, Z), x, c)

    def plane(n):
        return (g, z * S + n)

    def remote(src, dst, ss, rs, dev_id):
        cp = pltpu.make_async_remote_copy(
            src_ref=src, dst_ref=dst, send_sem=ss, recv_sem=rs, device_id=dev_id, device_id_type=MESH
        )
        cp.start()
        return cp

    loads = []
    for j in range(CH):
        cp = pltpu.make_async_copy(hist.at[:, pl.ds(j * RC, RC), :], hists[0][j], load_sem.at[j])
        cp.start()
        loads.append(cp)
    big = [
        pltpu.make_async_copy(tiles_hbm, tiles, in_sem.at[0]),
        pltpu.make_async_copy(inc_hbm, inc, in_sem.at[1]),
        pltpu.make_async_copy(jac_hbm, jac, in_sem.at[2]),
        pltpu.make_async_copy(self_hbm, selft, in_sem.at[3]),
    ]

    barrier = pltpu.get_barrier_semaphore()
    for dz in range(1, Z):
        pl.semaphore_signal(barrier, inc=1, device_id=zpeer(dz), device_id_type=MESH)
    for i in range(1, S):
        pl.semaphore_signal(barrier, inc=1, device_id=plane(lax.rem(me + i, S)), device_id_type=MESH)
    for i in range(1, G):
        pl.semaphore_signal(barrier, inc=1, device_id=(lax.rem(g + i, G), dev), device_id_type=MESH)
    pl.semaphore_wait(barrier, Z - 1 + S - 1 + G - 1)

    sent = []
    hops = {}

    def h1(j):
        loads[j].wait()
        for d, dz in ((0, 1), (1, -1)):
            hops[1, j, d] = remote(hists[0][j], hists[1 + d][j], h_s.at[0, j, d], h_r.at[0, j, d], zpeer(dz))

    def h2(j):
        for d, dz in ((0, 1), (1, -1)):
            hops[1, j, d].wait_recv()
            hops[2, j, d] = remote(hists[1 + d][j], hists[3 + d][j], h_s.at[1, j, d], h_r.at[1, j, d], zpeer(dz))

    def h3(j):
        for d, dz in ((0, 1), (1, -1)):
            hops[2, j, d].wait_recv()
            near = lax.rem(z + dz + Z, Z) * S
            far = lax.rem(z + 2 * dz + Z, Z) * S + d * (S // 2)

            @pl.loop(0, S)
            def _(n):
                fsel[d, j, n] = hists[3 + d][j][pl.ds(slag[3 + d, 0, near + n], STEPS)]

            @pl.loop(0, S // 2)
            def _(n):
                fsel[d, j, S + n] = hists[3 + d][j][pl.ds(slag[3 + d, 0, far + n], STEPS)]

            hops[3, j, d] = remote(fsel.at[d, j], pkt3.at[d, j], h_s.at[2, j, d], h_r.at[2, j, d], zpeer(dz))

    def xsend(j, pick, width, col):
        for i in range(1, S):
            n = lax.rem(me + i, S)
            remote(pick(n), recvs[j].at[pl.ds(me * Z + col, width)], x_s.at[j], x_r.at[j], plane(n))
        pltpu.make_async_copy(pick(me), recvs[j].at[pl.ds(me * Z + col, width)], x_r.at[j]).start()

    def xa(j):
        for o in range(5):

            @pl.loop(0, S)
            def _(n):
                sel[j, n, o] = hists[o][j][pl.ds(slag[o, 0, z * S + n], STEPS)]

        xsend(j, lambda n: sel.at[j, n], 5, 0)

    def h4(j):
        for d, dz in ((0, 1), (1, -1)):
            hops[3, j, d].wait_recv()
            hops[4, j, d] = remote(
                pkt3.at[d, j, pl.ds(S, S // 2)], pkt4.at[j, pl.ds(d * (S // 2), S // 2)],
                h_s.at[3, j, d], h_r.at[3, j, d], zpeer(dz),
            )
        for d in range(2):
            xsend(j, lambda n: pkt3.at[d, j, pl.ds(n, 1)], 1, 5 + d)

    def xb(j):
        for d in range(2):
            hops[4, j, d].wait_recv()
        xsend(j, lambda n: pkt4.at[j, pl.ds(n, 1)], 1, 7)

    def cross(j):
        @pl.loop(0, 2 * G)
        def _(n):
            csel[j, n] = hists[0][j][pl.ds(slag[0, 1, n], STEPS)]

        dst = recvs[j].at[pl.ds(Z * S + 2 * g, 2)]
        for i in range(1, G):
            h = lax.rem(g + i, G)
            remote(csel.at[j, pl.ds(2 * h, 2)], dst, x_s.at[j], x_r.at[j], (h, dev))
        pltpu.make_async_copy(csel.at[j, pl.ds(2 * g, 2)], dst, x_r.at[j]).start()

    def compute(j):
        pltpu.make_async_copy(recvs[j], recvs[j], x_r.at[j]).wait()
        cum[TILES] = jnp.zeros((ROWS, W), F32)

        def body(i, acc):
            v = recvs[j][ssrt[1, i]].reshape(ROWS, W)
            t = tiles[ssrt[0, i]]
            acc = acc * ssrt[2, i].astype(F32) + jnp.dot(v, t, preferred_element_type=F32)
            cum[i] = acc
            return acc

        lax.fori_loop(0, TILES, body, jnp.zeros((ROWS, W), F32), unroll=UNROLL)

    rs = {}

    def rs1(j):
        b = j % 2
        if j >= 2:
            rs[1, j - 2].wait_send()

        @pl.loop(0, X * Z)
        def _(n):
            e = (lax.rem(n, Z) * X + n // Z) * C + 1 - c
            send1[b, n] = cum[ssrt[3, e]].astype(SEND1)

        rs[1, j] = remote(send1.at[b], r1.at[j], rs_s.at[0, j, 0], rs_r.at[0, j, 0], at(z, x, 1 - c))

    def rs2(j):
        b = j % 2
        rs[1, j].wait_recv()
        if j >= 2:
            for i in range(1, X):
                rs[2, j - 2, i].wait_send()
        for i in range(1, X):
            xx = lax.rem(x + i, X)

            @pl.loop(0, Z)
            def _(n):
                total = cum[ssrt[3, (n * X + xx) * C + c]] + r1[j, xx * Z + n].astype(F32)
                send2[b, i - 1, n] = total.astype(SEND2)

            rs[2, j, i] = remote(
                send2.at[b, i - 1], r2.at[j, i - 1], rs_s.at[1, j, i], rs_r.at[1, j, i], at(z, xx, c)
            )

        @pl.loop(0, Z)
        def _(n):
            own2[b, n] = cum[ssrt[3, (n * X + x) * C + c]] + r1[j, x * Z + n].astype(F32)

    def rs3(j):
        b = j % 2
        for i in range(1, X):
            rs[2, j, i].wait_recv()
        if j >= 2:
            for i in range(1, Z):
                rs[3, j - 2, i].wait_send()
        for i in range(Z):
            n = lax.rem(z + i, Z)
            total = own2[b, n] + r2[j, 0, n].astype(F32) + r2[j, 1, n].astype(F32) + r2[j, 2, n].astype(F32)
            if i == 0:
                own3[b] = total
            else:
                send3[b, i - 1] = total.astype(SEND3)
                rs[3, j, i] = remote(
                    send3.at[b, i - 1], r3.at[j, i - 1], rs_s.at[2, j, i], rs_r.at[2, j, i], zpeer(i)
                )

    def rs4(j):
        b = j % 2
        total = own3[b]
        for i in range(1, Z):
            rs[3, j, i].wait_recv()
            total = total + r3[j, i - 1].astype(F32)
        rows = pl.ds(j * RC, RC)
        one, two = hists[0][j][0], hists[0][j][1]
        inverse = jac[...]
        for k in range(STEPS):
            part = total[(STEPS - 1 - k) * RC : (STEPS - k) * RC]
            term = jnp.dot(one, selft[0], preferred_element_type=F32)
            term = term + jnp.dot(two, selft[1], preferred_element_type=F32)
            resid = inc[k, rows] - part - term
            value = jnp.dot(resid, inverse, precision=lax.Precision.HIGHEST, preferred_element_type=F32)
            out[k, rows] = value
            two, one = one, value.astype(BF16)

    def order():
        lane = lax.broadcasted_iota(I32, (128, 128), 1)
        sub = lax.broadcasted_iota(I32, (128, 128), 0)
        by_lane = jnp.where(lane < TILES, jnp.broadcast_to(meta[3:4, :], (128, 128)), 127)
        by_sub = by_lane.T
        q = meta[2:3, :]
        dz = lax.rem(z - q // S + Z, Z)
        o = jnp.where(dz == 1, 1, 0)
        for d, place in ((7, 2), (2, 3), (6, 4), (3, 5), (5, 6), (4, 7)):
            o = jnp.where(dz == d, place, o)
        place = jnp.where(q < Z * S, lax.rem(q, S) * Z + o, q)
        place = jnp.broadcast_to(place, (128, 128)).T
        same = jnp.where((by_lane == by_sub) & (lane < sub), 1, 0)
        before = jnp.where(by_lane < by_sub, 1, 0) + same
        rank = jnp.sum(before, axis=1, keepdims=True)
        goes_on = jnp.where(jnp.sum(same, axis=1, keepdims=True) > 0, 1, 0)
        hot = jnp.where(rank == lane, 1, 0)
        upto = jnp.sum(jnp.where(by_sub <= lane, 1, 0), axis=0, keepdims=True)
        count = jnp.sum(jnp.where(by_sub == lane, 1, 0), axis=0, keepdims=True)
        srt[0:1, :] = jnp.sum(hot * sub, axis=0, keepdims=True)
        srt[1:2, :] = jnp.sum(hot * place, axis=0, keepdims=True)
        srt[2:3, :] = jnp.sum(hot * goes_on, axis=0, keepdims=True)
        srt[3:4, :] = jnp.where(count > 0, upto - 1, TILES)
        srt[4:8, :] = jnp.zeros((4, 128), I32)

    lags = []
    for i, dz in enumerate((1, -1, 2, -2)):
        lags.append(remote(meta, lagbuf.at[1 + i], lag_s.at[i], lag_r.at[i], zpeer(dz)))
    h1(0)
    h1(1)
    for cp in big:
        cp.start()
    lagbuf[0] = meta[...]
    order()
    for cp in lags:
        cp.wait_recv()
    cp = pltpu.make_async_copy(lagbuf, slag, small_sem.at[0])
    cp.start()
    cp2 = pltpu.make_async_copy(srt, ssrt, small_sem.at[1])
    cp2.start()
    cp.wait()
    cp2.wait()
    cross(0)
    cross(1)

    h2(0)
    h2(1)
    h3(0)
    h1(2)
    xa(0)
    h4(0)
    h3(1)
    xa(1)
    cross(2)
    h2(2)
    xb(0)
    h4(1)
    h1(3)
    h3(2)
    for cp in big:
        cp.wait()
    compute(0)
    rs1(0)
    xa(2)
    cross(3)
    h2(3)
    rs2(0)
    xb(1)
    h4(2)
    compute(1)
    rs1(1)
    rs3(0)
    h3(3)
    xa(3)
    rs2(1)
    xb(2)
    rs4(0)
    rs3(1)
    h4(3)
    compute(2)
    rs1(2)
    xb(3)
    rs2(2)
    rs4(1)
    compute(3)
    rs1(3)
    rs3(2)
    rs2(3)
    rs4(2)
    rs3(3)
    rs4(3)

    for cp in lags:
        cp.wait_send()
    for cp in hops.values():
        cp.wait_send()
    for j in range(CH):
        away = (S - 1) * Z + 2 * (G - 1)
        pltpu.make_async_copy(recvs[j].at[pl.ds(0, away)], recvs[j].at[pl.ds(0, away)], x_s.at[j]).wait()
    for j in range(CH - 2, CH):
        rs[1, j].wait_send()
        for i in range(1, X):
            rs[2, j, i].wait_send()
        for i in range(1, Z):
            rs[3, j, i].wait_send()


def per_device(
    history, incident, jacobi, self_tiles, near_tiles, send_lag, cross_lag, tile_slot, tile_dest
):
    def row(a):
        flat = a.reshape(1, -1)
        return jnp.pad(flat, ((0, 0), (0, 128 - flat.shape[1])))

    meta = jnp.concatenate(
        [row(send_lag - STEPS), row(cross_lag - STEPS), row(tile_slot), row(tile_dest), jnp.zeros((4, 128), I32)]
    )
    dma = pltpu.SemaphoreType.DMA
    hbm = pl.BlockSpec(memory_space=pl.ANY)
    vmem = pl.BlockSpec(memory_space=pltpu.VMEM)
    piece = (STEPS, RC, W)
    out = pl.pallas_call(
        kernel,
        out_shape=jax.ShapeDtypeStruct((STEPS, R, W), F32),
        in_specs=[vmem, hbm, hbm, hbm, hbm, hbm],
        out_specs=vmem,
        scratch_shapes=[
            [[pltpu.VMEM((LAGS, RC, W), BF16)] * CH] * 5,
            pltpu.VMEM((2, CH, S + S // 2, *piece), BF16),
            pltpu.VMEM((CH, S, *piece), BF16),
            pltpu.VMEM((2, CH, S + S // 2, *piece), BF16),
            pltpu.VMEM((CH, S, 5, *piece), BF16),
            pltpu.VMEM((CH, 2 * G, *piece), BF16),
            [pltpu.VMEM((SLOTS, *piece), BF16)] * CH,
            pltpu.VMEM((TILES, W, W), BF16),
            pltpu.VMEM((STEPS, R, W), F32),
            pltpu.VMEM((W, W), F32),
            pltpu.VMEM((2, W, W), BF16),
            pltpu.VMEM((TILES + 1, ROWS, W), F32),
            pltpu.VMEM((2, X * Z, ROWS, W), SEND1),
            pltpu.VMEM((CH, X * Z, ROWS, W), SEND1),
            pltpu.VMEM((2, X - 1, Z, ROWS, W), SEND2),
            pltpu.VMEM((2, Z, ROWS, W), F32),
            pltpu.VMEM((CH, X - 1, Z, ROWS, W), SEND2),
            pltpu.VMEM((2, Z - 1, ROWS, W), SEND3),
            pltpu.VMEM((2, ROWS, W), F32),
            pltpu.VMEM((CH, Z - 1, ROWS, W), SEND3),
            pltpu.VMEM((5, 8, 128), I32),
            pltpu.VMEM((8, 128), I32),
            pltpu.SMEM((5, 8, 128), I32),
            pltpu.SMEM((8, 128), I32),
            dma((CH,)),
            dma((4,)),
            dma((4,)),
            dma((4,)),
            dma((2,)),
            dma((4, CH, 2)),
            dma((4, CH, 2)),
            dma((CH,)),
            dma((CH,)),
            dma((3, CH, Z)),
            dma((3, CH, Z)),
        ],
        compiler_params=pltpu.CompilerParams(
            collective_id=0, has_side_effects=True, vmem_limit_bytes=62 * 2**20
        ),
    )(meta, history[0], incident[0], jacobi[0], self_tiles[0], near_tiles[0])
    return out[None]


def solution(mesh):
    spec = P(("group", "dev"))
    return jax.shard_map(
        per_device, mesh=mesh, in_specs=(spec,) * 9, out_specs=spec, check_vma=False
    )
```

```python
import functools

import jax
import jax.numpy as jnp
from jax import lax
from jax.experimental import pallas as pl
from jax.experimental.pallas import tpu as pltpu
from jax.sharding import PartitionSpec as P

MESH = pl.DeviceIdType.MESH
Z, X, C = 8, 4, 2
S = X * C
G = 4
LAGS, R, W, STEPS = 48, 64, 256, 3
TILES = 76
SLOTS = Z * S + 2 * G
CH = 4
RC = R // CH
ROWS = STEPS * RC
F32, BF16, I32 = jnp.float32, jnp.bfloat16, jnp.int32
SEND1, SEND2, SEND3 = F32, BF16, F32
UNROLL = 4
PIECES = 4
ZP = Z // PIECES


def kernel(
    send_lag, cross_lag, tile_slot, tile_dest, hist, inc_hbm, jac_hbm, self_hbm, tiles_hbm, out,
    hists, pkt3, pkt4, fsel, sel, csel, recvs, tiles, inc, jac, selft,
    cum, send1, r1, send2, own2, r2, send3, own3, r3,
    meta, lagbuf, srt, slag, ssrt,
    load_sem, in_sem, lag_s, lag_r, small_sem,
    h_s, h_r, x_s, x_r, rs_s, rs_r,
):
    dev, g = lax.axis_index("dev"), lax.axis_index("group")
    z, x, c = dev // S, (dev // C) % X, dev % C
    me = x * C + c

    def at(zz, xx, cc):
        return (g, (zz * X + xx) * C + cc)

    def zpeer(dz):
        return at(lax.rem(z + dz + Z, Z), x, c)

    def plane(n):
        return (g, z * S + n)

    def remote(src, dst, ss, rs, dev_id):
        cp = pltpu.make_async_remote_copy(
            src_ref=src, dst_ref=dst, send_sem=ss, recv_sem=rs, device_id=dev_id, device_id_type=MESH
        )
        cp.start()
        return cp

    loads = []
    for j in range(CH):
        cp = pltpu.make_async_copy(hist.at[:, pl.ds(j * RC, RC), :], hists[0][j], load_sem.at[j])
        cp.start()
        loads.append(cp)
    big = [
        pltpu.make_async_copy(tiles_hbm, tiles, in_sem.at[0]),
        pltpu.make_async_copy(inc_hbm, inc, in_sem.at[1]),
        pltpu.make_async_copy(jac_hbm, jac, in_sem.at[2]),
        pltpu.make_async_copy(self_hbm, selft, in_sem.at[3]),
    ]

    meta[...] = jnp.zeros((8, 128), I32)
    meta[0:1, 0 : Z * S] = jnp.maximum(send_lag[...] - STEPS, 0)
    meta[2:3, 0:TILES] = tile_slot[...]
    meta[3:4, 0:TILES] = tile_dest[...]
    meta[4 : 4 + G, 0:2] = jnp.maximum(cross_lag[...] - STEPS, 0)

    barrier = pltpu.get_barrier_semaphore()
    for dz in range(1, Z):
        pl.semaphore_signal(barrier, inc=1, device_id=zpeer(dz), device_id_type=MESH)
    for i in range(1, S):
        pl.semaphore_signal(barrier, inc=1, device_id=plane(lax.rem(me + i, S)), device_id_type=MESH)
    for i in range(1, G):
        pl.semaphore_signal(barrier, inc=1, device_id=(lax.rem(g + i, G), dev), device_id_type=MESH)
    pl.semaphore_wait(barrier, Z - 1 + S - 1 + G - 1)

    sent = []
    hops = {}

    def h1(j):
        for d, dz in ((0, 1), (1, -1)):
            hops[1, j, d] = remote(hists[0][j], hists[1 + d][j], h_s.at[0, j, d], h_r.at[0, j, d], zpeer(dz))

    def h2(j):
        for d, dz in ((0, 1), (1, -1)):
            hops[1, j, d].wait_recv()
            hops[2, j, d] = remote(hists[1 + d][j], hists[3 + d][j], h_s.at[1, j, d], h_r.at[1, j, d], zpeer(dz))

    def h3(j):
        for d, dz in ((0, 1), (1, -1)):
            hops[2, j, d].wait_recv()
            near = lax.rem(z + dz + Z, Z) * S
            far = lax.rem(z + 2 * dz + Z, Z) * S + d * (S // 2)

            @pl.loop(0, S)
            def _(n):
                fsel[d, j, n] = hists[3 + d][j][pl.ds(slag[3 + d, 0, near + n], STEPS)]

            @pl.loop(0, S // 2)
            def _(n):
                fsel[d, j, S + n] = hists[3 + d][j][pl.ds(slag[3 + d, 0, far + n], STEPS)]

            hops[3, j, d] = remote(fsel.at[d, j], pkt3.at[d, j], h_s.at[2, j, d], h_r.at[2, j, d], zpeer(dz))

    def xsend(j, pick, width, col):
        for i in range(1, S):
            n = lax.rem(me + i, S)
            remote(pick(n), recvs[j].at[pl.ds(me * Z + col, width)], x_s.at[j], x_r.at[j], plane(n))
        pltpu.make_async_copy(pick(me), recvs[j].at[pl.ds(me * Z + col, width)], x_r.at[j]).start()

    def xa(j, lo, hi):
        for o in range(lo, hi):

            @pl.loop(0, S)
            def _(n):
                sel[j, n, o] = hists[o][j][pl.ds(slag[o, 0, z * S + n], STEPS)]

        xsend(j, lambda n: sel.at[j, n, pl.ds(lo, hi - lo)], hi - lo, lo)

    def h4(j):
        for d, dz in ((0, 1), (1, -1)):
            hops[3, j, d].wait_recv()
            hops[4, j, d] = remote(
                pkt3.at[d, j, pl.ds(S, S // 2)], pkt4.at[j, pl.ds(d * (S // 2), S // 2)],
                h_s.at[3, j, d], h_r.at[3, j, d], zpeer(dz),
            )
        for d in range(2):
            xsend(j, lambda n: pkt3.at[d, j, pl.ds(n, 1)], 1, 5 + d)

    def xb(j):
        for d in range(2):
            hops[4, j, d].wait_recv()
        xsend(j, lambda n: pkt4.at[j, pl.ds(n, 1)], 1, 7)

    def cross(j):
        @pl.loop(0, 2 * G)
        def _(n):
            csel[j, n] = hists[0][j][pl.ds(slag[0, 4 + n // 2, lax.rem(n, 2)], STEPS)]

        dst = recvs[j].at[pl.ds(Z * S + 2 * g, 2)]
        for i in range(1, G):
            h = lax.rem(g + i, G)
            remote(csel.at[j, pl.ds(2 * h, 2)], dst, x_s.at[j], x_r.at[j], (h, dev))
        pltpu.make_async_copy(csel.at[j, pl.ds(2 * g, 2)], dst, x_r.at[j]).start()

    def compute(j):
        pltpu.make_async_copy(recvs[j], recvs[j], x_r.at[j]).wait()
        cum[TILES] = jnp.zeros((ROWS, W), F32)

        def body(i, acc):
            v = recvs[j][ssrt[1, i]].reshape(ROWS, W)
            t = tiles[ssrt[0, i]]
            acc = acc * ssrt[2, i].astype(F32) + jnp.dot(v, t, preferred_element_type=F32)
            cum[i] = acc
            return acc

        lax.fori_loop(0, TILES, body, jnp.zeros((ROWS, W), F32), unroll=UNROLL)

    rs = {}

    def rs1(j):
        b = j % 2
        if j >= 2:
            for p in range(PIECES):
                rs[1, j - 2, p].wait_send()
        for p in range(PIECES):

            @pl.loop(0, X * ZP)
            def _(n):
                e = (lax.rem(z + 1 + p * ZP + lax.rem(n, ZP), Z) * X + n // ZP) * C + 1 - c
                send1[b, p, n] = cum[ssrt[3, e]].astype(SEND1)

            rs[1, j, p] = remote(
                send1.at[b, p], r1.at[j, p], rs_s.at[0, j, p], rs_r.at[0, j, p], at(z, x, 1 - c)
            )

    def rs2(j, p):
        b = j % 2
        rs[1, j, p].wait_recv()
        if j >= 2:
            for i in range(1, X):
                rs[2, j - 2, p, i].wait_send()

        def total(xx, n):
            zz = lax.rem(z + 1 + p * ZP + n, Z)
            return cum[ssrt[3, (zz * X + xx) * C + c]] + r1[j, p, xx * ZP + n].astype(F32)

        for i in range(1, X):
            xx = lax.rem(x + i, X)
            for n in range(ZP):
                send2[b, p, i - 1, n] = total(xx, n).astype(SEND2)
            q = p * X + i
            rs[2, j, p, i] = remote(
                send2.at[b, p, i - 1], r2.at[j, p, i - 1], rs_s.at[1, j, q], rs_r.at[1, j, q], at(z, xx, c)
            )
        for n in range(ZP):
            own2[b, p, n] = total(x, n)

    def rs3(j, p):
        b = j % 2
        for i in range(1, X):
            rs[2, j, p, i].wait_recv()
        for n in range(ZP):
            i = p * ZP + n
            total = own2[b, p, n]
            for k in range(X - 1):
                total = total + r2[j, p, k, n].astype(F32)
            if i == Z - 1:
                own3[j] = total
            else:
                if j >= 2:
                    rs[3, j - 2, i].wait_send()
                send3[b, i] = total.astype(SEND3)
                rs[3, j, i] = remote(send3.at[b, i], r3.at[j, i], rs_s.at[2, j, i], rs_r.at[2, j, i], zpeer(i + 1))

    def rs4(j):
        rows = pl.ds(j * RC, RC)
        first, second = selft[0], selft[1]
        one, two = hists[0][j][0], hists[0][j][1]

        def dot(u, v):
            return jnp.dot(u, v, preferred_element_type=F32)

        known = [dot(one, first) + dot(two, second), dot(one, second)]
        total = own3[j]
        for i in range(Z - 1):
            rs[3, j, i].wait_recv()
            total = total + r3[j, i].astype(F32)
        inverse = jac[...]
        past = []
        for k in range(STEPS):
            term = known[k] if k < 2 else dot(past[k - 2], second)
            if k > 0:
                term = term + dot(past[k - 1], first)
            resid = inc[k, rows] - total[(STEPS - 1 - k) * RC : (STEPS - k) * RC] - term
            value = jnp.dot(resid, inverse, precision=lax.Precision.HIGHEST, preferred_element_type=F32)
            out[k, rows] = value
            past.append(value.astype(BF16))

    def order():
        lane = lax.broadcasted_iota(I32, (128, 128), 1)
        sub = lax.broadcasted_iota(I32, (128, 128), 0)
        by_lane = jnp.where(lane < TILES, jnp.broadcast_to(meta[3:4, :], (128, 128)), 127)
        by_sub = by_lane.T
        q = meta[2:3, :]
        dz = lax.rem(z - q // S + Z, Z)
        o = jnp.where(dz == 1, 1, 0)
        for d, place in ((7, 2), (2, 3), (6, 4), (3, 5), (5, 6), (4, 7)):
            o = jnp.where(dz == d, place, o)
        place = jnp.where(q < Z * S, lax.rem(q, S) * Z + o, q)
        place = jnp.broadcast_to(place, (128, 128)).T
        same = jnp.where((by_lane == by_sub) & (lane < sub), 1, 0)
        before = jnp.where(by_lane < by_sub, 1, 0) + same
        rank = jnp.sum(before, axis=1, keepdims=True)
        goes_on = jnp.where(jnp.sum(same, axis=1, keepdims=True) > 0, 1, 0)
        hot = jnp.where(rank == lane, 1, 0)
        upto = jnp.sum(jnp.where(by_sub <= lane, 1, 0), axis=0, keepdims=True)
        count = jnp.sum(jnp.where(by_sub == lane, 1, 0), axis=0, keepdims=True)
        srt[0:1, :] = jnp.sum(hot * sub, axis=0, keepdims=True)
        srt[1:2, :] = jnp.sum(hot * place, axis=0, keepdims=True)
        srt[2:3, :] = jnp.sum(hot * goes_on, axis=0, keepdims=True)
        srt[3:4, :] = jnp.where(count > 0, upto - 1, TILES)
        srt[4:8, :] = jnp.zeros((4, 128), I32)

    for cp in loads:
        cp.wait()
    lags = []
    for i, dz in enumerate((1, -1, 2, -2)):
        lags.append(remote(meta, lagbuf.at[1 + i], lag_s.at[i], lag_r.at[i], zpeer(dz)))
    h1(0)
    h1(1)
    for cp in big:
        cp.start()
    lagbuf[0] = meta[...]
    order()
    for cp in lags:
        cp.wait_recv()
    cp = pltpu.make_async_copy(lagbuf, slag, small_sem.at[0])
    cp.start()
    cp2 = pltpu.make_async_copy(srt, ssrt, small_sem.at[1])
    cp2.start()
    cp.wait()
    cp2.wait()
    cross(0)
    cross(1)

    xa(0, 0, 1)
    xa(1, 0, 1)
    h2(0)
    xa(0, 1, 3)
    h2(1)
    xa(1, 1, 3)
    h3(0)
    h1(2)
    xa(0, 3, 5)
    xa(2, 0, 1)
    xa(3, 0, 1)
    h4(0)
    h3(1)
    xa(1, 3, 5)
    cross(2)
    cross(3)
    h2(2)
    xa(2, 1, 3)
    xb(0)
    h4(1)
    h1(3)
    h3(2)
    xa(2, 3, 5)
    for cp in big:
        cp.wait()
    compute(0)
    rs1(0)
    h2(3)
    xa(3, 1, 3)
    for p in range(PIECES):
        rs2(0, p)
    xb(1)
    h4(2)
    compute(1)
    rs1(1)
    for p in range(PIECES):
        rs3(0, p)
    h3(3)
    xa(3, 3, 5)
    for p in range(PIECES):
        rs2(1, p)
    xb(2)
    rs4(0)
    for p in range(PIECES):
        rs3(1, p)
    h4(3)
    compute(2)
    rs1(2)
    xb(3)
    for p in range(PIECES):
        rs2(2, p)
    rs4(1)
    compute(3)
    rs1(3)
    for p in range(PIECES):
        rs3(2, p)
    rs2(3, 0)
    rs2(3, 1)
    rs3(3, 0)
    rs2(3, 2)
    rs3(3, 1)
    rs2(3, 3)
    rs3(3, 2)
    rs3(3, 3)
    rs4(2)
    rs4(3)
    for cp in lags:
        cp.wait_send()
    for cp in hops.values():
        cp.wait_send()
    for j in range(CH):
        away = (S - 1) * Z + 2 * (G - 1)
        pltpu.make_async_copy(recvs[j].at[pl.ds(0, away)], recvs[j].at[pl.ds(0, away)], x_s.at[j]).wait()
    for j in range(CH - 2, CH):
        for p in range(PIECES):
            rs[1, j, p].wait_send()
            for i in range(1, X):
                rs[2, j, p, i].wait_send()
        for i in range(Z - 1):
            rs[3, j, i].wait_send()


def per_device(
    history, incident, jacobi, self_tiles, near_tiles, send_lag, cross_lag, tile_slot, tile_dest
):
    dma = pltpu.SemaphoreType.DMA
    hbm = pl.BlockSpec(memory_space=pl.ANY)
    vmem = pl.BlockSpec(memory_space=pltpu.VMEM)
    piece = (STEPS, RC, W)
    out = pl.pallas_call(
        kernel,
        out_shape=jax.ShapeDtypeStruct((STEPS, R, W), F32),
        in_specs=[vmem] * 4 + [hbm] * 5,
        out_specs=vmem,
        scratch_shapes=[
            [[pltpu.VMEM((LAGS, RC, W), BF16)] * CH] * 5,
            pltpu.VMEM((2, CH, S + S // 2, *piece), BF16),
            pltpu.VMEM((CH, S, *piece), BF16),
            pltpu.VMEM((2, CH, S + S // 2, *piece), BF16),
            pltpu.VMEM((CH, S, 5, *piece), BF16),
            pltpu.VMEM((CH, 2 * G, *piece), BF16),
            [pltpu.VMEM((SLOTS, *piece), BF16)] * CH,
            pltpu.VMEM((TILES, W, W), BF16),
            pltpu.VMEM((STEPS, R, W), F32),
            pltpu.VMEM((W, W), F32),
            pltpu.VMEM((2, W, W), BF16),
            pltpu.VMEM((TILES + 1, ROWS, W), F32),
            pltpu.VMEM((2, PIECES, X * ZP, ROWS, W), SEND1),
            pltpu.VMEM((CH, PIECES, X * ZP, ROWS, W), SEND1),
            pltpu.VMEM((2, PIECES, X - 1, ZP, ROWS, W), SEND2),
            pltpu.VMEM((2, PIECES, ZP, ROWS, W), F32),
            pltpu.VMEM((CH, PIECES, X - 1, ZP, ROWS, W), SEND2),
            pltpu.VMEM((2, Z - 1, ROWS, W), SEND3),
            pltpu.VMEM((CH, ROWS, W), F32),
            pltpu.VMEM((CH, Z - 1, ROWS, W), SEND3),
            pltpu.VMEM((8, 128), I32),
            pltpu.VMEM((5, 8, 128), I32),
            pltpu.VMEM((8, 128), I32),
            pltpu.SMEM((5, 8, 128), I32),
            pltpu.SMEM((8, 128), I32),
            dma((CH,)),
            dma((4,)),
            dma((4,)),
            dma((4,)),
            dma((2,)),
            dma((4, CH, 2)),
            dma((4, CH, 2)),
            dma((CH,)),
            dma((CH,)),
            dma((3, CH, PIECES * X)),
            dma((3, CH, PIECES * X)),
        ],
        compiler_params=pltpu.CompilerParams(
            collective_id=0, has_side_effects=True, vmem_limit_bytes=62 * 2**20
        ),
    )(
        send_lag.reshape(1, -1), cross_lag[0], tile_slot, tile_dest, history[0], incident[0], jacobi[0], self_tiles[0], near_tiles[0]
    )
    return out[None]


def solution(mesh):
    spec = P(("group", "dev"))
    return jax.shard_map(
        per_device, mesh=mesh, in_specs=(spec,) * 9, out_specs=spec, check_vma=False
    )
```
